256 devices in a mesh: row: 16 (over y, x_lo, core), col: 16 (over x_hi, z).
Axes of the slice: x: 4 (x_hi: 2, x_lo: 2; x = x_hi * 2 + x_lo), y: 4, z: 8, core: 2. Of those that a mesh axis runs over, the one named last changes fastest.
Arguments:
- iterate: bfloat16 [5632, 9216], P('row', 'col'), may hold values from -0.046875 to 0.046875
Outputs:
- update: bfloat16 [5632, 9216], P('row', 'col')
The draws below stay inside these ranges and needn't reach their ends.
All inputs are finite; a program needn't handle non-finite values.
Results may differ from the reference program's by a relative error of at most 0.0065.
Values may be sent and summed in bfloat16 or wider, within the bound.
No kernel may reach another device: no remote copies, remote signals or barrier semaphores. Data moves between devices by JAX's collectives and lax.ppermute only.
A program may use at most 64 MiB of HBM per device.

```python
import math
import jax
import jax.numpy as jnp

D = 5632
F = 9216


def block_scale(key, shape, shards, low, top_value):
    loudness, own = 1.0, jax.random.fold_in(key, 6)
    for axis_at, blocks in shards:
        draws = jnp.exp(jax.random.uniform(jax.random.fold_in(own, axis_at), (blocks,), jnp.float32, low / len(shards), top_value / len(shards)))
        loudness = loudness * jnp.repeat(draws, shape[axis_at] // blocks).reshape([-1 if axis == axis_at else 1 for axis in range(len(shape))])
    return loudness


def scatter_about(own_key, dims, spread, limit, cuts=(), dtype=jnp.bfloat16):
    factor_of = block_scale(own_key, dims, cuts, -0.22, 0.18) if cuts else 1.0
    drawn = jax.random.normal(own_key, dims, jnp.float32) * spread * factor_of
    return jnp.minimum(jnp.maximum(drawn, -limit), limit).astype(dtype)


def setup_inputs(seed: int = 0) -> dict:
    streams_of = jax.random.split(jax.random.key(seed), 2)
    iterate = scatter_about(streams_of[0], (D, F), (2 * F) ** -0.5, 0.046875, ((0, 16), (1, 16)))
    return dict(iterate=iterate)


first_term = 3.4445
third_term = -4.775
fifth_term = 2.0315

def reference(iterate):
    gram_float = jnp.dot(iterate, iterate.T, preferred_element_type=jnp.float32)
    gram_half = gram_float.astype(jnp.bfloat16)
    square_term = jnp.dot(gram_half, gram_half, preferred_element_type=jnp.float32)
    poly_half = (third_term * gram_float + fifth_term * square_term).astype(jnp.bfloat16)
    mixed_sum = jnp.dot(poly_half, iterate, preferred_element_type=jnp.float32)
    update_scale = 0.2 * math.sqrt(max(D, F))
    return (update_scale * (first_term * iterate.astype(jnp.float32) + mixed_sum)).astype(jnp.bfloat16)
```

```python
import functools
import math

import jax
import jax.numpy as jnp
from jax import lax
from jax.experimental import pallas as pl
from jax.experimental.pallas import tpu as pltpu
from jax.sharding import Mesh
from jax.sharding import PartitionSpec as P

D = 5632
F = 9216

first_term = 3.4445
third_term = -4.775
fifth_term = 2.0315

SIZES = {"y": 4, "xl": 2, "core": 2, "xh": 2, "z": 8}
ROW = ("y", "xl", "core")
COL = ("xh", "z")
VMEM = 56 * 2**20


def shift(value, axis, by):
    n = SIZES[axis]
    return lax.ppermute(value, axis, [(i, (i + by) % n) for i in range(n)])


def row_gather(own):
    got = {(0, 0): own}
    got[3, 0] = shift(own, "y", 1)
    got[1, 0] = shift(own, "y", -1)
    got[0, 1] = shift(own, "xl", 1)
    got[2, 0] = shift(own, "y", 2)
    got[3, 1] = shift(got[3, 0], "xl", 1)
    got[1, 1] = shift(got[1, 0], "xl", 1)
    got[2, 1] = shift(got[0, 1], "y", 2)
    blocks = [None] * 16
    for (dy, dxl), block in got.items():
        blocks[dy * 4 + dxl * 2] = block
        blocks[dy * 4 + dxl * 2 + 1] = shift(block, "core", 1)
    return blocks


def slots():
    at = {name: lax.axis_index(name) for name in SIZES}
    h, d = jnp.arange(16) // 8, jnp.arange(16) % 8
    k = (at["xh"] + h) % 2 * 8 + (at["z"] + d) % 8
    dy = (k // 4 - at["y"]) % 4
    dxl = (k // 2 - at["xl"]) % 2
    dcore = (k - at["core"]) % 2
    return (dy * 4 + dxl * 2 + dcore).astype(jnp.int32)


def load_all(pairs, sem):
    copies = [pltpu.make_async_copy(src, dst, sem.at[i]) for i, (src, dst) in enumerate(pairs)]
    for copy in copies:
        copy.start()
    for copy in copies:
        copy.wait()


def gram_kernel(half, idx, own, *refs):
    blocks, outs, (stack, sem) = refs[:16], refs[16:-2], refs[-2:]
    load_all([(blocks[i], stack.at[i]) for i in range(16)], sem)
    mine, upper, swapped, lower = outs[0], outs[1:9], outs[9], outs[10:]
    for h in range(2):
        for d in range(8):
            tile = jnp.dot(own[...], stack[idx[h * 8 + d]], preferred_element_type=jnp.float32)
            if h == 0 and d == 0:
                mine[...] = tile
            else:
                tile = tile.astype(jnp.bfloat16)
                upper[d][h] = tile[:half]
                if h:
                    swapped[d] = tile[half:]
                elif d:
                    lower[d - 1][...] = tile[half:]


def gram_tiles(idx, own, blocks):
    n, m = own.shape
    half = n // 2
    bf = jnp.bfloat16
    vmem = pl.BlockSpec(memory_space=pltpu.VMEM)
    out_shape = (
        [jax.ShapeDtypeStruct((n, n), jnp.float32)]
        + [jax.ShapeDtypeStruct((2, half, n), bf)] * 8
        + [jax.ShapeDtypeStruct((8, half, n), bf)]
        + [jax.ShapeDtypeStruct((half, n), bf)] * 7
    )
    outs = pl.pallas_call(
        functools.partial(gram_kernel, half),
        out_shape=out_shape,
        in_specs=[pl.BlockSpec(memory_space=pltpu.SMEM), vmem] + [pl.BlockSpec(memory_space=pl.ANY)] * 16,
        out_specs=[vmem] * len(out_shape),
        scratch_shapes=[pltpu.VMEM((16, m, n), bf), pltpu.SemaphoreType.DMA((16,))],
        compiler_params=pltpu.CompilerParams(vmem_limit_bytes=VMEM),
        cost_estimate=pl.CostEstimate(flops=32 * n * n * m, bytes_accessed=20_000_000, transcendentals=0),
    )(idx, own, *blocks)
    return outs[0], outs[1:9], outs[9], (None, *outs[10:])


def add(*terms):
    return sum(t.astype(jnp.float32) for t in terms)


def half_add(*terms):
    return add(*terms).astype(jnp.bfloat16)


def col_scatter(mine, upper, swapped, lower):
    half = mine.shape[0] // 2
    other = shift(swapped, "xh", 1)
    plus = shift(upper[4][0], "z", 1)
    minus = shift(upper[4][1], "z", -1)
    plus = shift(jnp.stack([half_add(upper[3][0], plus), upper[3][1]]), "z", 1)
    minus = shift(jnp.stack([upper[5][0], half_add(upper[5][1], minus)]), "z", -1)
    for d in (2, 1):
        plus = shift(half_add(upper[d], plus), "z", 1)
        minus = shift(half_add(upper[8 - d], minus), "z", -1)
    crossed = shift(half_add(upper[0][1], plus[1], minus[1]), "xh", 1)
    low_plus = shift(half_add(lower[4], other[4]), "z", 1)
    low_minus = shift(half_add(lower[5], other[5]), "z", -1)
    for d in (3, 2, 1):
        low_plus = shift(half_add(lower[d], other[d], low_plus), "z", 1)
        if d < 3:
            low_minus = shift(half_add(lower[8 - d], other[8 - d], low_minus), "z", -1)
    top = mine[:half] + add(plus[0], minus[0], crossed)
    bottom = mine[half:] + add(other[0], low_plus, low_minus)
    return jnp.concatenate([top, bottom])


def col_gather(tile):
    half = tile.shape[0] // 2
    upper, lower = tile[:half], tile[half:]
    pair = jnp.stack([upper, shift(upper, "xh", 1)])
    low = [lower] + [None] * 7
    high = [pair] + [None] * 7
    for s in (1, 2, 3, 4):
        low[8 - s] = shift(low[(9 - s) % 8], "z", 1)
        if s < 4:
            low[s] = shift(low[s - 1], "z", -1)
    for s in (1, 2, 3):
        high[8 - s] = shift(high[(9 - s) % 8], "z", 1)
        high[s] = shift(high[s - 1], "z", -1)
    far = shift(high[5][0], "z", 1), shift(high[3][1], "z", -1)
    low_other = [shift(t, "xh", 1) for t in low]
    return high[:4] + high[5:], far, low, low_other


def product_kernel(half, last, idx, *refs):
    blocks, high, refs = refs[:16], refs[16:23], refs[23:]
    far, low, low_other, refs = refs[:2], refs[2:10], refs[10:18], refs[18:]
    if last:
        x, y, out, refs = refs[0], refs[1], refs[2], refs[3:]
    else:
        y, y_half, refs = refs[0], refs[1], refs[2:]
    left, right, acc, sem = refs
    top, bottom = pl.ds(0, half), pl.ds(half, half)
    pairs = [(blocks[i], left.at[i]) for i in range(16)]
    for i, d in enumerate((0, 1, 2, 3, 5, 6, 7)):
        for h in range(2):
            pairs.append((high[i].at[h], right.at[h * 8 + d, top]))
    for h in range(2):
        pairs.append((far[h], right.at[h * 8 + 4, top]))
    for d in range(8):
        pairs.append((low[d], right.at[d, bottom]))
        pairs.append((low_other[d], right.at[8 + d, bottom]))
    load_all(pairs, sem)
    acc[...] = jnp.zeros_like(acc)
    for j in range(16):
        acc[...] += jnp.dot(left[idx[j]], right[j], preferred_element_type=jnp.float32)
    if last:
        scale = 0.2 * math.sqrt(max(D, F))
        total = first_term * x[...].astype(jnp.float32) + third_term * y[...] + fifth_term * acc[...]
        out[...] = (scale * total).astype(out.dtype)
    else:
        y[...] = acc[...]
        y_half[...] = acc[...].astype(y_half.dtype)


def product(idx, blocks, gram, x=None, y=None):
    high, far, low, low_other = gram
    m, n = blocks[0].shape
    half = n // 2
    bf = jnp.bfloat16
    last = x is not None
    vmem = pl.BlockSpec(memory_space=pltpu.VMEM)
    hbm = pl.BlockSpec(memory_space=pl.ANY)
    pieces = [*blocks, *high, *far, *low, *low_other]
    whole = [jax.ShapeDtypeStruct((m, n), jnp.float32), jax.ShapeDtypeStruct((m, n), bf)]
    return pl.pallas_call(
        functools.partial(product_kernel, half, last),
        out_shape=whole[1] if last else whole,
        in_specs=[pl.BlockSpec(memory_space=pltpu.SMEM)] + [hbm] * len(pieces) + [vmem] * (2 * last),
        out_specs=vmem if last else [vmem] * 2,
        scratch_shapes=[
            pltpu.VMEM((16, m, n), bf),
            pltpu.VMEM((16, n, n), bf),
            pltpu.VMEM((m, n), jnp.float32),
            pltpu.SemaphoreType.DMA((48,)),
        ],
        compiler_params=pltpu.CompilerParams(vmem_limit_bytes=VMEM),
        cost_estimate=pl.CostEstimate(flops=32 * n * n * m, bytes_accessed=14_000_000, transcendentals=0),
    )(idx, *pieces, *((x, y) if last else ()))


def body(iterate):
    xt = iterate.T
    idx = slots()
    blocks = row_gather(xt)
    tile = col_scatter(*gram_tiles(idx, iterate, blocks))
    gram = col_gather(tile.T.astype(jnp.bfloat16))
    y, y_half = product(idx, blocks, gram)
    return product(idx, row_gather(y_half), gram, xt, y).T


def solution(mesh):
    split = Mesh(mesh.devices.reshape(tuple(SIZES.values())), tuple(SIZES))
    spec = P(ROW, COL)
    return jax.shard_map(body, mesh=split, in_specs=(spec,), out_specs=spec, check_vma=False)
```

```python
import functools
import math

import jax
import jax.numpy as jnp
from jax import lax
from jax.experimental import pallas as pl
from jax.experimental.pallas import tpu as pltpu
from jax.sharding import Mesh
from jax.sharding import PartitionSpec as P

D = 5632
F = 9216

first_term = 3.4445
third_term = -4.775
fifth_term = 2.0315

SIZES = {"y": 4, "xl": 2, "core": 2, "xh": 2, "z": 8}
ROW = ("y", "xl", "core")
COL = ("xh", "z")
VMEM = 32 * 2**20
BF = jnp.bfloat16
CUT = 256

SMEM_SPEC = pl.BlockSpec(memory_space=pltpu.SMEM)
VMEM_SPEC = pl.BlockSpec(memory_space=pltpu.VMEM)
ANY_SPEC = pl.BlockSpec(memory_space=pl.ANY)


def shift(value, axis, by):
    n = SIZES[axis]
    return lax.ppermute(value, axis, [(i, (i + by) % n) for i in range(n)])


def row_gather(own):
    got = {(0, 0): own}
    got[3, 0] = shift(own, "y", 1)
    got[1, 0] = shift(own, "y", -1)
    got[0, 1] = shift(own, "xl", 1)
    got[2, 0] = shift(own, "y", 2)
    got[3, 1] = shift(got[3, 0], "xl", 1)
    got[1, 1] = shift(got[1, 0], "xl", 1)
    got[2, 1] = shift(got[0, 1], "y", 2)
    blocks = []
    for dxl in range(2):
        blocks.append([])
        for dy in range(4):
            blocks[dxl] += [got[dy, dxl], shift(got[dy, dxl], "core", 1)]
    return blocks


def start_all(pairs, sem):
    copies = [pltpu.make_async_copy(src, dst, sem.at[i]) for i, (src, dst) in enumerate(pairs)]
    for copy in copies:
        copy.start()
    return copies


def gram_kernel(at, own, *refs):
    blocks, outs, (stack, sem) = refs[:8], refs[8:16], refs[16:]
    for copy in start_all([(blocks[i], stack.at[i]) for i in range(8)], sem):
        copy.wait()
    for d in range(8):
        slot = lax.rem(at[0] + d, 8)
        tile = jnp.dot(own[...], stack[slot], preferred_element_type=jnp.float32)
        outs[d][...] = tile.astype(outs[d].dtype)


def gram_tiles(z, own, blocks):
    n, m = own.shape
    return pl.pallas_call(
        gram_kernel,
        out_shape=[jax.ShapeDtypeStruct((n, n), BF if d else jnp.float32) for d in range(8)],
        in_specs=[SMEM_SPEC, VMEM_SPEC] + [ANY_SPEC] * 8,
        out_specs=[VMEM_SPEC] * 8,
        scratch_shapes=[pltpu.VMEM((8, m, n), BF), pltpu.SemaphoreType.DMA((8,))],
        compiler_params=pltpu.CompilerParams(vmem_limit_bytes=VMEM),
        cost_estimate=pl.CostEstimate(flops=16 * n * n * m, bytes_accessed=10_000_000, transcendentals=0),
    )(z, own, *blocks)


def add(*terms):
    return sum(t.astype(jnp.float32) for t in terms)


def ring_sum(tiles, far_up):
    up, down = None, None
    for d in (4, 3, 2, 1):
        if d < 4 or far_up:
            up = tiles[d] if up is None else add(tiles[d], up).astype(BF)
            up = shift(up, "z", 1)
        if d < 4 or not far_up:
            down = tiles[8 - d] if down is None else add(tiles[8 - d], down).astype(BF)
            down = shift(down, "z", -1)
    return add(tiles[0], up, down)


def ring_gather(pair):
    got = [pair] + [None] * 7
    for s in (1, 2, 3):
        got[8 - s] = shift(got[(9 - s) % 8], "z", 1)
        got[s] = shift(got[s - 1], "z", -1)
    return got[:4] + got[5:], [shift(got[5][0], "z", 1), shift(got[3][1], "z", -1)]


def load_gram(slots, pairs, far, dst):
    copies = []
    for i, d in enumerate((0, 1, 2, 3, 5, 6, 7)):
        for h in range(2):
            copies.append((pairs[i].at[h], dst.at[slots[h * 8 + d]]))
    for h in range(2):
        copies.append((far[h], dst.at[slots[h * 8 + 4]]))
    return copies


def first_kernel(slots, *refs):
    blocks, pairs, far, refs = refs[:16], refs[16:23], refs[23:25], refs[25:]
    y, y_half, gram, left, sem, gram_sem = refs
    copies = start_all(load_gram(slots, pairs, far, gram), gram_sem)
    loads = start_all([(blocks[i], left.at[i]) for i in range(16)], sem)
    for copy in copies:
        copy.wait()
    for j in range(16):
        loads[j].wait()
        part = jnp.dot(left[j], gram[j], preferred_element_type=jnp.float32)
        if j == 0:
            y[...] = part
        else:
            y[...] += part
    y_half[...] = y[...].astype(BF)


def first_product(slots, blocks, pairs, far):
    m, n = blocks[0].shape
    w = pairs[0].shape[-1]
    return pl.pallas_call(
        first_kernel,
        out_shape=[
            jax.ShapeDtypeStruct((m, w), jnp.float32),
            jax.ShapeDtypeStruct((m, w), BF),
            jax.ShapeDtypeStruct((16, n, w), BF),
        ],
        in_specs=[SMEM_SPEC] + [ANY_SPEC] * 25,
        out_specs=[VMEM_SPEC] * 3,
        scratch_shapes=[pltpu.VMEM((16, m, n), BF), pltpu.SemaphoreType.DMA((16,)), pltpu.SemaphoreType.DMA((16,))],
        compiler_params=pltpu.CompilerParams(vmem_limit_bytes=VMEM),
        cost_estimate=pl.CostEstimate(flops=32 * n * w * m, bytes_accessed=12_000_000, transcendentals=0),
    )(slots, *blocks, *pairs, *far)


def last_kernel(rows, final, *refs):
    blocks, grams, refs = refs[:16], refs[16:18], refs[18:]
    if final:
        x, y_a, y_b, acc_a, acc_b, out, refs = *refs[:6], refs[6:]
    else:
        sum_a, sum_b, refs = *refs[:2], refs[2:]
    left, right_a, right_b, sem, gram_sem = refs
    loads = start_all([(blocks[i], left.at[i]) for i in range(16)], sem)
    copies = start_all(
        [(g.at[:, pl.ds(rows[0], rows[1])], r) for g, r in zip(grams, (right_a, right_b))], gram_sem
    )
    for copy in copies:
        copy.wait()
    sums = []
    for right in (right_a, right_b):
        total = None
        for j in range(16):
            if right is right_a:
                loads[j].wait()
            part = jnp.dot(left[j], right[j], preferred_element_type=jnp.float32)
            total = part if total is None else total + part
        sums.append(total)
    if final:
        scale = 0.2 * math.sqrt(max(D, F))
        for total, acc, y, at in ((sums[0], acc_a, y_a, pl.ds(0, CUT)), (sums[1], acc_b, y_b, pl.ds(CUT, y_b.shape[1]))):
            square = acc[...] + total
            mixed = first_term * x[:, at].astype(jnp.float32) + third_term * y[...] + fifth_term * square
            out[:, at] = (scale * mixed).astype(out.dtype)
    else:
        sum_a[...], sum_b[...] = sums


def last_product(blocks, grams, start, extra=()):
    m, w = blocks[0].shape
    widths = [g.shape[-1] for g in grams]
    final = bool(extra)
    shapes = [jax.ShapeDtypeStruct((m, v), jnp.float32) for v in widths]
    return pl.pallas_call(
        functools.partial(last_kernel, (start, w), final),
        out_shape=jax.ShapeDtypeStruct((m, sum(widths)), BF) if final else shapes,
        in_specs=[ANY_SPEC] * 18 + [VMEM_SPEC] * len(extra),
        out_specs=VMEM_SPEC if final else [VMEM_SPEC] * 2,
        scratch_shapes=[
            pltpu.VMEM((16, m, w), BF),
            pltpu.VMEM((16, w, widths[0]), BF),
            pltpu.VMEM((16, w, widths[1]), BF),
            pltpu.SemaphoreType.DMA((16,)),
            pltpu.SemaphoreType.DMA((2,)),
        ],
        compiler_params=pltpu.CompilerParams(vmem_limit_bytes=VMEM),
        cost_estimate=pl.CostEstimate(flops=32 * w * sum(widths) * m, bytes_accessed=12_000_000, transcendentals=0),
    )(*blocks, *grams, *extra)


def body(iterate):
    xt = iterate.T
    xh, z = lax.axis_index("xh"), lax.axis_index("z")
    j = jnp.arange(16)
    slots = ((xh + j // 8) % 2 * 8 + (z + j % 8) % 8).astype(jnp.int32)
    z_ref = jnp.reshape(z, (1,)).astype(jnp.int32)

    blocks = row_gather(xt)
    sums = [ring_sum(gram_tiles(z_ref, iterate, blocks[s]), s == 0) for s in range(2)]
    low = xh == 0
    away = jnp.where(low, sums[1], sums[0]).astype(BF)
    tile = jnp.where(low, sums[0], sums[1]) + shift(away, "xh", 1).astype(jnp.float32)
    tile = tile.T.astype(BF)
    pair = jnp.stack([tile, shift(tile, "xh", 1)])
    blocks = blocks[0] + blocks[1]
    y_a, half_a, gram_a = first_product(slots, blocks, *ring_gather(pair[:, :, :CUT]))
    y_b, half_b, gram_b = first_product(slots, blocks, *ring_gather(pair[:, :, CUT:]))
    got = row_gather(half_a)
    sums = last_product(got[0] + got[1], (gram_a, gram_b), 0)
    got = row_gather(half_b)
    return last_product(got[0] + got[1], (gram_a, gram_b), CUT, (xt, y_a, y_b, *sums)).T


def solution(mesh):
    split = Mesh(mesh.devices.reshape(tuple(SIZES.values())), tuple(SIZES))
    spec = P(ROW, COL)
    return jax.shard_map(body, mesh=split, in_specs=(spec,), out_specs=spec, check_vma=False)
```

```python
import functools
import math

import jax
import jax.numpy as jnp
from jax import lax
from jax.experimental import pallas as pl
from jax.experimental.pallas import tpu as pltpu
from jax.sharding import Mesh
from jax.sharding import PartitionSpec as P

D = 5632
F = 9216

first_term = 3.4445
third_term = -4.775
fifth_term = 2.0315

SIZES = {"y": 4, "xl": 2, "core": 2, "xh": 2, "z": 8}
ROW = ("y", "xl", "core")
COL = ("xh", "z")
BF = jnp.bfloat16
CUT = 256

SMEM_SPEC = pl.BlockSpec(memory_space=pltpu.SMEM)
VMEM_SPEC = pl.BlockSpec(memory_space=pltpu.VMEM)
ANY_SPEC = pl.BlockSpec(memory_space=pl.ANY)
LAST_DIMS = (((1,), (1,)), ((), ()))


def params(mib):
    return pltpu.CompilerParams(vmem_limit_bytes=mib * 2**20)


def shift(value, axis, by):
    n = SIZES[axis]
    return lax.ppermute(value, axis, [(i, (i + by) % n) for i in range(n)])


def row_gather(own):
    got = {(0, 0): own}
    got[3, 0] = shift(own, "y", 1)
    got[1, 0] = shift(own, "y", -1)
    got[0, 1] = shift(own, "xl", 1)
    got[2, 0] = shift(own, "y", 2)
    got[3, 1] = shift(got[3, 0], "xl", 1)
    got[1, 1] = shift(got[1, 0], "xl", 1)
    got[2, 1] = shift(got[0, 1], "y", 2)
    blocks = []
    for dxl in range(2):
        for dy in range(4):
            blocks += [got[dy, dxl], shift(got[dy, dxl], "core", 1)]
    return blocks


def gram_kernel(at, own, *refs):
    blocks, outs, hold = refs[:16], refs[16:-1], refs[-1]
    for j in range(16):
        tile = jnp.dot(own[...], blocks[j][...], preferred_element_type=jnp.float32)
        hold[lax.rem(j % 8 + 8 - at[0], 8), j // 8] = tile.astype(BF)
    chunks = ((outs[:9], pl.ds(0, CUT)), (outs[9:], pl.ds(CUT, own.shape[0] - CUT)))
    for to, rows in chunks:
        for i, d in enumerate((0, 1, 2, 3, 5, 6, 7)):
            to[i][...] = hold[d, :, rows, :]
        for h in range(2):
            to[7 + h][...] = hold[4, h, rows, :]


def gram_tiles(z, own, blocks):
    n, m = own.shape
    out_shape = []
    for rows in (CUT, n - CUT):
        out_shape += [jax.ShapeDtypeStruct((2, rows, n), BF)] * 7 + [jax.ShapeDtypeStruct((rows, n), BF)] * 2
    outs = pl.pallas_call(
        gram_kernel,
        out_shape=out_shape,
        in_specs=[SMEM_SPEC] + [VMEM_SPEC] * 17,
        out_specs=[VMEM_SPEC] * 18,
        scratch_shapes=[pltpu.VMEM((8, 2, n, n), BF)],
        compiler_params=params(22),
        cost_estimate=pl.CostEstimate(flops=32 * n * n * m, bytes_accessed=10_000_000, transcendentals=0),
    )(z, own, *blocks)
    return outs[:9], outs[9:]


def add(*terms):
    return sum(t.astype(jnp.float32) for t in terms)


def ring_sum(tiles):
    near, far_up, far_down = dict(zip((0, 1, 2, 3, 5, 6, 7), tiles[:7])), tiles[7], tiles[8]
    up, down = shift(far_up, "z", 1), shift(far_down, "z", -1)
    up = jnp.stack([add(near[3][0], up).astype(BF), near[3][1]])
    down = jnp.stack([near[5][0], add(near[5][1], down).astype(BF)])
    up, down = shift(up, "z", 1), shift(down, "z", -1)
    for d in (2, 1):
        up = shift(add(near[d], up).astype(BF), "z", 1)
        down = shift(add(near[8 - d], down).astype(BF), "z", -1)
    total = add(near[0], up, down)
    return (total + shift(total.astype(BF), "xh", 1).astype(jnp.float32)).astype(BF)


def ring_gather(pair):
    got = [pair] + [None] * 7
    for s in (1, 2, 3):
        got[8 - s] = shift(got[(9 - s) % 8], "z", 1)
        got[s] = shift(got[s - 1], "z", -1)
    return got[:4] + got[5:] + [shift(got[5][0], "z", 1), shift(got[3][1], "z", -1)]


def first_kernel(at, *refs):
    blocks, tiles, refs = refs[:16], refs[16:25], refs[25:]
    y, y_half, gram, sem = refs
    pairs = []
    for i, d in enumerate((0, 1, 2, 3, 5, 6, 7)):
        for h in range(2):
            pairs.append((tiles[i].at[h], gram.at[h * 8 + lax.rem(at[0] + d, 8)]))
    for h in range(2):
        pairs.append((tiles[7 + h], gram.at[h * 8 + lax.rem(at[0] + 4, 8)]))
    copies = [pltpu.make_async_copy(src, dst, sem.at[i]) for i, (src, dst) in enumerate(pairs)]
    for copy in copies:
        copy.start()
    for copy in copies:
        copy.wait()
    total = None
    for j in range(16):
        part = lax.dot_general(blocks[j][...], gram[j], LAST_DIMS, preferred_element_type=jnp.float32)
        total = part if total is None else total + part
    y[...] = total
    y_half[...] = total.astype(BF)


def first_product(z, blocks, tiles):
    m, n = blocks[0].shape
    w = tiles[0].shape[1]
    return pl.pallas_call(
        first_kernel,
        out_shape=[
            jax.ShapeDtypeStruct((m, w), jnp.float32),
            jax.ShapeDtypeStruct((m, w), BF),
            jax.ShapeDtypeStruct((16, w, n), BF),
        ],
        in_specs=[SMEM_SPEC] + [VMEM_SPEC] * 16 + [ANY_SPEC] * 9,
        out_specs=[VMEM_SPEC] * 3,
        scratch_shapes=[pltpu.SemaphoreType.DMA((16,))],
        compiler_params=params(20),
        cost_estimate=pl.CostEstimate(flops=32 * n * w * m, bytes_accessed=10_000_000, transcendentals=0),
    )(z, *blocks, *tiles)


def last_kernel(lanes, final, *refs):
    blocks, grams, refs = refs[:16], refs[16:18], refs[18:]
    sums = []
    for gram in grams:
        total = None
        for j in range(16):
            part = lax.dot_general(
                blocks[j][...], gram[j, :, lanes], LAST_DIMS, preferred_element_type=jnp.float32
            )
            total = part if total is None else total + part
        sums.append(total)
    if final:
        x, y_a, y_b, acc_a, acc_b, out = refs
        scale = 0.2 * math.sqrt(max(D, F))
        for total, acc, y, at in ((sums[0], acc_a, y_a, pl.ds(0, CUT)), (sums[1], acc_b, y_b, pl.ds(CUT, y_b.shape[1]))):
            square = acc[...] + total
            mixed = first_term * x[:, at].astype(jnp.float32) + third_term * y[...] + fifth_term * square
            out[:, at] = (scale * mixed).astype(out.dtype)
    else:
        refs[0][...], refs[1][...] = sums


def last_product(blocks, grams, start, extra=()):
    m, w = blocks[0].shape
    widths = [g.shape[1] for g in grams]
    final = bool(extra)
    shapes = [jax.ShapeDtypeStruct((m, v), jnp.float32) for v in widths]
    return pl.pallas_call(
        functools.partial(last_kernel, pl.ds(start, w), final),
        out_shape=jax.ShapeDtypeStruct((m, sum(widths)), BF) if final else shapes,
        in_specs=[VMEM_SPEC] * (18 + len(extra)),
        out_specs=VMEM_SPEC if final else [VMEM_SPEC] * 2,
        compiler_params=params(20),
        cost_estimate=pl.CostEstimate(flops=32 * w * sum(widths) * m, bytes_accessed=10_000_000, transcendentals=0),
    )(*blocks, *grams, *extra)


def body(iterate):
    xt = iterate.T
    z = jnp.reshape(lax.axis_index("z"), (1,)).astype(jnp.int32)
    blocks = row_gather(xt)
    tiles_a, tiles_b = gram_tiles(z, iterate, blocks)
    y_a, half_a, gram_a = first_product(z, blocks, ring_gather(ring_sum(tiles_a)))
    y_b, half_b, gram_b = first_product(z, blocks, ring_gather(ring_sum(tiles_b)))
    grams = (gram_a, gram_b)
    sums = last_product(row_gather(half_a), grams, 0)
    return last_product(row_gather(half_b), grams, CUT, (xt, y_a, y_b, *sums)).T


def solution(mesh):
    split = Mesh(mesh.devices.reshape(tuple(SIZES.values())), tuple(SIZES))
    spec = P(ROW, COL)
    return jax.shard_map(body, mesh=split, in_specs=(spec,), out_specs=spec, check_vma=False)
```

```python
import functools
import math

import jax
import jax.numpy as jnp
from jax import lax
from jax.experimental import pallas as pl
from jax.experimental.pallas import tpu as pltpu
from jax.sharding import Mesh
from jax.sharding import PartitionSpec as P

D = 5632
F = 9216

first_term = 3.4445
third_term = -4.775
fifth_term = 2.0315

SIZES = {"y": 4, "xl": 2, "core": 2, "xh": 2, "z": 8}
ROW = ("y", "xl", "core")
COL = ("xh", "z")
BF = jnp.bfloat16
CUT = 256

SMEM_SPEC = pl.BlockSpec(memory_space=pltpu.SMEM)
VMEM_SPEC = pl.BlockSpec(memory_space=pltpu.VMEM)
ANY_SPEC = pl.BlockSpec(memory_space=pl.ANY)
NEAR = (0, 1, 2, 3, 5, 6, 7)
EARLY = [(0, 0), (1, 0), (3, 0), (0, 1)]
ORDER = EARLY + [(2, 0), (1, 1), (3, 1), (2, 1)]
FIRST = [(*at, dcore) for at in EARLY for dcore in range(2)]
SECOND = [(*at, dcore) for at in ORDER[4:] for dcore in range(2)]
LAST_DIMS = (((1,), (1,)), ((), ()))


def params(mib):
    return pltpu.CompilerParams(vmem_limit_bytes=mib * 2**20)


def shift(value, axis, by):
    n = SIZES[axis]
    return lax.ppermute(value, axis, [(i, (i + by) % n) for i in range(n)])


def after(values, *marks):
    return lax.optimization_barrier((*values, *marks))[: len(values)]


def row_gather(own):
    got = {(0, 0): own}
    up, down = shift(own, "y", 1), shift(own, "y", -1)
    got[3, 0], got[1, 0] = up, down
    got[0, 1] = shift(own, "xl", 1)
    got[3, 1], got[1, 1] = shift(up, "xl", 1), shift(down, "xl", 1)
    here, across = after((own, got[0, 1]), up, down)
    got[2, 0], got[2, 1] = shift(here, "y", 2), shift(across, "y", 2)
    held = dict(zip(EARLY, after([got[at] for at in EARLY], got[2, 0])))
    blocks = {}
    for at in ORDER:
        blocks[*at, 0] = got[at]
        blocks[*at, 1] = shift(held.get(at, got[at]), "core", 1)
    return blocks


def by_slot(blocks):
    return [blocks[dy, dxl, dcore] for dxl in range(2) for dy in range(4) for dcore in range(2)]


def early_kernel(own, *refs):
    blocks, out = refs[:-1], refs[-1]
    for i, block in enumerate(blocks):
        out[i] = jnp.dot(own[...], block[...], preferred_element_type=jnp.float32).astype(BF)


def late_kernel(at, own, done, *refs):
    blocks, outs, hold = refs[:-19], refs[-19:-1], refs[-1]
    tiles = [done[i] for i in range(done.shape[0])]
    for block in blocks:
        tiles.append(jnp.dot(own[...], block[...], preferred_element_type=jnp.float32).astype(BF))
    for i, (dy, dxl, dcore) in enumerate(FIRST + SECOND):
        hold[lax.rem(dy * 2 + dcore + 8 - at[0], 8), dxl] = tiles[i]
    chunks = ((outs[:9], pl.ds(0, CUT)), (outs[9:], pl.ds(CUT, own.shape[0] - CUT)))
    for to, rows in chunks:
        for i, d in enumerate(NEAR):
            to[i][...] = hold[d, :, rows, :]
        for h in range(2):
            to[7 + h][...] = hold[4, h, rows, :]


def gram_tiles(z, own, blocks):
    n, m = own.shape
    out_shape = []
    for rows in (CUT, n - CUT):
        out_shape += [jax.ShapeDtypeStruct((2, rows, n), BF)] * 7 + [jax.ShapeDtypeStruct((rows, n), BF)] * 2
    cost = pl.CostEstimate(flops=16 * n * n * m, bytes_accessed=10_000_000, transcendentals=0)
    done = pl.pallas_call(
        early_kernel,
        out_shape=jax.ShapeDtypeStruct((len(FIRST), n, n), BF),
        in_specs=[VMEM_SPEC] * (1 + len(FIRST)),
        out_specs=VMEM_SPEC,
        compiler_params=params(16),
        cost_estimate=cost,
    )(own, *[blocks[at] for at in FIRST])
    outs = pl.pallas_call(
        late_kernel,
        out_shape=out_shape,
        in_specs=[SMEM_SPEC] + [VMEM_SPEC] * (2 + len(SECOND)),
        out_specs=[VMEM_SPEC] * 18,
        scratch_shapes=[pltpu.VMEM((8, 2, n, n), BF)],
        compiler_params=params(22),
        cost_estimate=cost,
    )(z, own, done, *[blocks[at] for at in SECOND])
    return outs[:9], outs[9:]


def add(*terms):
    return sum(t.astype(jnp.float32) for t in terms)


def ring_sum(tiles, marks=()):
    near, far_up, far_down = dict(zip(NEAR, tiles[:7])), tiles[7], tiles[8]
    far_up, far_down = after((far_up, far_down), *marks)
    up, down = shift(far_up, "z", 1), shift(far_down, "z", -1)
    marks = up, down
    up = jnp.stack([add(near[3][0], up).astype(BF), near[3][1]])
    down = jnp.stack([near[5][0], add(near[5][1], down).astype(BF)])
    up, down = shift(up, "z", 1), shift(down, "z", -1)
    for d in (2, 1):
        up = shift(add(near[d], up).astype(BF), "z", 1)
        down = shift(add(near[8 - d], down).astype(BF), "z", -1)
    total = add(near[0], up, down)
    return (total + shift(total.astype(BF), "xh", 1).astype(jnp.float32)).astype(BF), marks


def ring_gather(pair):
    got = [pair] + [None] * 7
    for s in (1, 2, 3):
        got[8 - s] = shift(got[(9 - s) % 8], "z", 1)
        got[s] = shift(got[s - 1], "z", -1)
    return got[:4] + got[5:] + [shift(got[5][0], "z", 1), shift(got[3][1], "z", -1)], (got[7], got[1])


def nt(left, right):
    return lax.dot_general(left, right, LAST_DIMS, preferred_element_type=jnp.float32)


def near_kernel(at, *refs):
    blocks, tiles, (y, gram, sem) = refs[:16], refs[16:23], refs[23:]
    pairs = []
    for i, d in enumerate(NEAR):
        for h in range(2):
            pairs.append((tiles[i].at[h], gram.at[h * 8 + lax.rem(at[0] + d, 8)]))
    copies = [pltpu.make_async_copy(src, dst, sem.at[i]) for i, (src, dst) in enumerate(pairs)]
    for copy in copies:
        copy.start()
    for h in range(2):
        gram[h * 8 + lax.rem(at[0] + 4, 8)] = jnp.zeros(gram.shape[1:], BF)
    for copy in copies:
        copy.wait()
    total = None
    for j in range(16):
        part = nt(blocks[j][...], gram[j])
        total = part if total is None else total + part
    y[...] = total


def far_kernel(at, *refs):
    blocks, (far_0, far_1, part, y, y_half) = refs[:16], refs[16:]
    for j in range(8):

        @pl.when(lax.rem(at[0] + 4, 8) == j)
        def _():
            total = part[...] + nt(blocks[j][...], far_0[...]) + nt(blocks[8 + j][...], far_1[...])
            y[...] = total
            y_half[...] = total.astype(BF)


def first_product(z, blocks, tiles):
    m, n = blocks[0].shape
    w = tiles[0].shape[1]
    part, gram = pl.pallas_call(
        near_kernel,
        out_shape=[jax.ShapeDtypeStruct((m, w), jnp.float32), jax.ShapeDtypeStruct((16, w, n), BF)],
        in_specs=[SMEM_SPEC] + [VMEM_SPEC] * 16 + [ANY_SPEC] * 7,
        out_specs=[VMEM_SPEC] * 2,
        scratch_shapes=[pltpu.SemaphoreType.DMA((14,))],
        compiler_params=params(20),
        cost_estimate=pl.CostEstimate(flops=32 * n * w * m, bytes_accessed=10_000_000, transcendentals=0),
    )(z, *blocks, *tiles[:7])
    y, y_half = pl.pallas_call(
        far_kernel,
        out_shape=[jax.ShapeDtypeStruct((m, w), jnp.float32), jax.ShapeDtypeStruct((m, w), BF)],
        in_specs=[SMEM_SPEC] + [VMEM_SPEC] * 19,
        out_specs=[VMEM_SPEC] * 2,
        compiler_params=params(20),
        cost_estimate=pl.CostEstimate(flops=4 * n * w * m, bytes_accessed=3_000_000, transcendentals=0),
    )(z, *blocks, *tiles[7:], part)
    return y, y_half, (gram, *tiles[7:])


def last_kernel(lanes, final, at, *refs):
    blocks, grams, refs = refs[:16], (refs[16:19], refs[19:22]), refs[22:]
    sums = []
    for gram, *far in grams:
        total = None
        for j in range(16):
            is_far = lax.rem(at[0] + 4, 8) == j % 8
            right = jnp.where(is_far, far[j // 8][:, lanes], gram[j, :, lanes])
            part = nt(blocks[j][...], right)
            total = part if total is None else total + part
        sums.append(total)
    if final:
        x, y_a, y_b, acc_a, acc_b, out = refs
        scale = 0.2 * math.sqrt(max(D, F))
        for total, acc, y, cols in ((sums[0], acc_a, y_a, pl.ds(0, CUT)), (sums[1], acc_b, y_b, pl.ds(CUT, y_b.shape[1]))):
            square = acc[...] + total
            mixed = first_term * x[:, cols].astype(jnp.float32) + third_term * y[...] + fifth_term * square
            out[:, cols] = (scale * mixed).astype(out.dtype)
    else:
        refs[0][...], refs[1][...] = sums


def last_product(z, blocks, grams, start, extra=()):
    m, w = blocks[0].shape
    widths = [g[0].shape[1] for g in grams]
    final = bool(extra)
    shapes = [jax.ShapeDtypeStruct((m, v), jnp.float32) for v in widths]
    return pl.pallas_call(
        functools.partial(last_kernel, pl.ds(start, w), final),
        out_shape=jax.ShapeDtypeStruct((m, sum(widths)), BF) if final else shapes,
        in_specs=[SMEM_SPEC] + [VMEM_SPEC] * (22 + len(extra)),
        out_specs=VMEM_SPEC if final else [VMEM_SPEC] * 2,
        compiler_params=params(20),
        cost_estimate=pl.CostEstimate(flops=32 * w * sum(widths) * m, bytes_accessed=10_000_000, transcendentals=0),
    )(z, *blocks, *grams[0], *grams[1], *extra)


def body(iterate):
    xt = iterate.T
    z = jnp.reshape(lax.axis_index("z"), (1,)).astype(jnp.int32)
    blocks = row_gather(xt)
    tiles_a, tiles_b = gram_tiles(z, iterate, blocks)
    blocks = by_slot(blocks)
    sum_a, marks = ring_sum(tiles_a)
    sum_b, _ = ring_sum(tiles_b, marks)
    all_a, marks = ring_gather(sum_a)
    all_b, _ = ring_gather(after((sum_b,), *marks)[0])
    y_a, half_a, gram_a = first_product(z, blocks, all_a)
    y_b, half_b, gram_b = first_product(z, blocks, all_b)
    grams = (gram_a, gram_b)
    got_a = row_gather(half_a)
    got_b = row_gather(after((half_b,), got_a[2, 0, 0])[0])
    sums = last_product(z, by_slot(got_a), grams, 0)
    return last_product(z, by_slot(got_b), grams, CUT, (xt, y_a, y_b, *sums)).T


def solution(mesh):
    split = Mesh(mesh.devices.reshape(tuple(SIZES.values())), tuple(SIZES))
    spec = P(ROW, COL)
    return jax.shard_map(body, mesh=split, in_specs=(spec,), out_specs=spec, check_vma=False)
```

```python
import functools
import math

import jax
import jax.numpy as jnp
from jax import lax
from jax.experimental import pallas as pl
from jax.experimental.pallas import tpu as pltpu
from jax.sharding import Mesh
from jax.sharding import PartitionSpec as P

D = 5632
F = 9216

first_term = 3.4445
third_term = -4.775
fifth_term = 2.0315

SIZES = {"y": 4, "xl": 2, "core": 2, "xh": 2, "z": 8}
ROW = ("y", "xl", "core")
COL = ("xh", "z")
BF = jnp.bfloat16
CUT = 256

SMEM_SPEC = pl.BlockSpec(memory_space=pltpu.SMEM)
VMEM_SPEC = pl.BlockSpec(memory_space=pltpu.VMEM)
NEAR = (0, 1, 2, 3, 5, 6, 7)
EARLY = [(0, 0), (1, 0), (3, 0), (0, 1)]
ORDER = EARLY + [(2, 0), (1, 1), (3, 1), (2, 1)]
FIRST = [(*at, dcore) for at in EARLY for dcore in range(2)]
SECOND = [(*at, dcore) for at in ORDER[4:] for dcore in range(2)]
LAST_DIMS = (((1,), (1,)), ((), ()))


def params(mib):
    return pltpu.CompilerParams(vmem_limit_bytes=mib * 2**20)


def shift(value, axis, by):
    n = SIZES[axis]
    return lax.ppermute(value, axis, [(i, (i + by) % n) for i in range(n)])


def after(values, *marks):
    return lax.optimization_barrier((*values, *marks))[: len(values)]


def row_gather(own):
    got = {(0, 0): own}
    up, down = shift(own, "y", 1), shift(own, "y", -1)
    got[3, 0], got[1, 0] = up, down
    got[0, 1] = shift(own, "xl", 1)
    got[3, 1], got[1, 1] = shift(up, "xl", 1), shift(down, "xl", 1)
    here, across = after((own, got[0, 1]), up, down)
    got[2, 0], got[2, 1] = shift(here, "y", 2), shift(across, "y", 2)
    blocks = {(*at, 0): got[at] for at in ORDER}
    for at, block in zip(EARLY, after([got[at] for at in EARLY], got[2, 0])):
        blocks[*at, 1] = shift(block, "core", 1)
    for at in ORDER[4:]:
        blocks[*at, 1] = shift(got[at], "core", 1)
    return blocks


def by_slot(blocks):
    return [blocks[dy, dxl, dcore] for dxl in range(2) for dy in range(4) for dcore in range(2)]


def tn(left, right):
    return lax.dot_general(left, right, (((0,), (0,)), ((), ())), preferred_element_type=jnp.float32)


def early_kernel(own, *refs):
    blocks, out = refs[:-1], refs[-1]
    for i, block in enumerate(blocks):
        out[i] = tn(own[...], block[...]).astype(BF)


def late_kernel(at, own, done, *refs):
    blocks, outs, hold = refs[:-19], refs[-19:-1], refs[-1]
    tiles = [done[i] for i in range(done.shape[0])]
    for block in blocks:
        tiles.append(tn(own[...], block[...]).astype(BF))
    for i, (dy, dxl, dcore) in enumerate(FIRST + SECOND):
        hold[lax.rem(dy * 2 + dcore + 8 - at[0], 8), dxl] = tiles[i]
    chunks = ((outs[:9], pl.ds(0, CUT)), (outs[9:], pl.ds(CUT, own.shape[1] - CUT)))
    for to, rows in chunks:
        for i, d in enumerate(NEAR):
            to[i][...] = hold[d, :, rows, :]
        for h in range(2):
            to[7 + h][...] = hold[4, h, rows, :]


def gram_cost(n, m):
    return pl.CostEstimate(flops=16 * n * n * m, bytes_accessed=10_000_000, transcendentals=0)


def early_tiles(own, blocks):
    m, n = own.shape
    return pl.pallas_call(
        early_kernel,
        out_shape=jax.ShapeDtypeStruct((len(blocks), n, n), BF),
        in_specs=[VMEM_SPEC] * (1 + len(blocks)),
        out_specs=VMEM_SPEC,
        compiler_params=params(16),
        cost_estimate=gram_cost(n, m),
    )(own, *blocks)


def gram_tiles(z, own, done, blocks):
    m, n = own.shape
    out_shape = []
    for rows in (CUT, n - CUT):
        out_shape += [jax.ShapeDtypeStruct((2, rows, n), BF)] * 7 + [jax.ShapeDtypeStruct((rows, n), BF)] * 2
    outs = pl.pallas_call(
        late_kernel,
        out_shape=out_shape,
        in_specs=[SMEM_SPEC] + [VMEM_SPEC] * (2 + len(blocks)),
        out_specs=[VMEM_SPEC] * 18,
        scratch_shapes=[pltpu.VMEM((8, 2, n, n), BF)],
        compiler_params=params(22),
        cost_estimate=gram_cost(n, m),
    )(z, own, done, *blocks)
    return outs[:9], outs[9:]


def add(*terms):
    return sum(t.astype(jnp.float32) for t in terms)


def ring_sum(tiles):
    near, far_up, far_down = dict(zip(NEAR, tiles[:7])), tiles[7], tiles[8]
    up, down = shift(far_up, "z", 1), shift(far_down, "z", -1)
    up = jnp.stack([add(near[3][0], up).astype(BF), near[3][1]])
    down = jnp.stack([near[5][0], add(near[5][1], down).astype(BF)])
    up, down = shift(up, "z", 1), shift(down, "z", -1)
    for d in (2, 1):
        up = shift(add(near[d], up).astype(BF), "z", 1)
        down = shift(add(near[8 - d], down).astype(BF), "z", -1)
    total = add(near[0], up, down)
    return (total + shift(total.astype(BF), "xh", 1).astype(jnp.float32)).astype(BF)


def ring_gather(pair):
    got = [pair] + [None] * 7
    for s in (1, 2, 3):
        got[8 - s] = shift(got[(9 - s) % 8], "z", 1)
        got[s] = shift(got[s - 1], "z", -1)
    return got[:4] + got[5:] + [shift(got[5][0], "z", 1), shift(got[3][1], "z", -1)], (got[7], got[1])


def nt(left, right):
    return lax.dot_general(left, right, LAST_DIMS, preferred_element_type=jnp.float32)


def near_kernel(at, *refs):
    blocks, tiles, (y, gram) = refs[:16], refs[16:23], refs[23:]
    for h in range(2):
        for i, d in enumerate(NEAR):
            gram[h * 8 + lax.rem(at[0] + d, 8)] = tiles[i][h]
        gram[h * 8 + lax.rem(at[0] + 4, 8)] = jnp.zeros(gram.shape[1:], BF)
    total = None
    for j in range(16):
        part = nt(blocks[j][...], gram[j])
        total = part if total is None else total + part
    y[...] = total


def far_kernel(at, *refs):
    blocks, (far_0, far_1, part, y, y_half) = refs[:16], refs[16:]
    for j in range(8):

        @pl.when(lax.rem(at[0] + 4, 8) == j)
        def _():
            total = part[...] + nt(blocks[j][...], far_0[...]) + nt(blocks[8 + j][...], far_1[...])
            y[...] = total
            y_half[...] = total.astype(BF)


def first_product(z, blocks, tiles):
    m, n = blocks[0].shape
    w = tiles[0].shape[1]
    part, gram = pl.pallas_call(
        near_kernel,
        out_shape=[jax.ShapeDtypeStruct((m, w), jnp.float32), jax.ShapeDtypeStruct((16, w, n), BF)],
        in_specs=[SMEM_SPEC] + [VMEM_SPEC] * 23,
        out_specs=[VMEM_SPEC] * 2,
        compiler_params=params(20),
        cost_estimate=pl.CostEstimate(flops=32 * n * w * m, bytes_accessed=10_000_000, transcendentals=0),
    )(z, *blocks, *tiles[:7])
    y, y_half = pl.pallas_call(
        far_kernel,
        out_shape=[jax.ShapeDtypeStruct((m, w), jnp.float32), jax.ShapeDtypeStruct((m, w), BF)],
        in_specs=[SMEM_SPEC] + [VMEM_SPEC] * 19,
        out_specs=[VMEM_SPEC] * 2,
        compiler_params=params(20),
        cost_estimate=pl.CostEstimate(flops=4 * n * w * m, bytes_accessed=3_000_000, transcendentals=0),
    )(z, *blocks, *tiles[7:], part)
    return y, y_half, (gram, *tiles[7:])


def last_kernel(lanes, final, at, *refs):
    blocks, grams, refs = refs[:16], (refs[16:19], refs[19:22]), refs[22:]
    sums = []
    for gram, *far in grams:
        total = None
        for j in range(16):
            is_far = lax.rem(at[0] + 4, 8) == j % 8
            right = jnp.where(is_far, far[j // 8][:, lanes], gram[j, :, lanes])
            part = nt(blocks[j][...], right)
            total = part if total is None else total + part
        sums.append(total)
    if final:
        x, y_a, y_b, acc_a, acc_b, out = refs
        scale = 0.2 * math.sqrt(max(D, F))
        for total, acc, y, cols in ((sums[0], acc_a, y_a, pl.ds(0, CUT)), (sums[1], acc_b, y_b, pl.ds(CUT, y_b.shape[1]))):
            square = acc[...] + total
            mixed = first_term * x[:, cols].astype(jnp.float32) + third_term * y[...] + fifth_term * square
            out[:, cols] = (scale * mixed).astype(out.dtype)
    else:
        refs[0][...], refs[1][...] = sums


def last_product(z, blocks, grams, start, extra=()):
    m, w = blocks[0].shape
    widths = [g[0].shape[1] for g in grams]
    final = bool(extra)
    shapes = [jax.ShapeDtypeStruct((m, v), jnp.float32) for v in widths]
    return pl.pallas_call(
        functools.partial(last_kernel, pl.ds(start, w), final),
        out_shape=jax.ShapeDtypeStruct((m, sum(widths)), BF) if final else shapes,
        in_specs=[SMEM_SPEC] + [VMEM_SPEC] * (22 + len(extra)),
        out_specs=VMEM_SPEC if final else [VMEM_SPEC] * 2,
        compiler_params=params(20),
        cost_estimate=pl.CostEstimate(flops=32 * w * sum(widths) * m, bytes_accessed=10_000_000, transcendentals=0),
    )(z, *blocks, *grams[0], *grams[1], *extra)


def body(iterate):
    xt = iterate.T
    z = jnp.reshape(lax.axis_index("z"), (1,)).astype(jnp.int32)
    blocks = row_gather(xt)
    done = early_tiles(xt, [blocks[at] for at in FIRST])
    tiles_a, tiles_b = gram_tiles(z, xt, done, [blocks[at] for at in SECOND])
    blocks = by_slot(blocks)
    sum_a = ring_sum(tiles_a)
    sum_b = ring_sum(tiles_b)
    all_a, marks = ring_gather(sum_a)
    all_b, _ = ring_gather(after((sum_b,), *marks)[0])
    y_a, half_a, gram_a = first_product(z, blocks, all_a)
    y_b, half_b, gram_b = first_product(z, blocks, all_b)
    grams = (gram_a, gram_b)
    got_a = row_gather(half_a)
    got_b = row_gather(after((half_b,), got_a[2, 0, 0])[0])
    sums = last_product(z, by_slot(got_a), grams, 0)
    return last_product(z, by_slot(got_b), grams, CUT, (xt, y_a, y_b, *sums)).T


def solution(mesh):
    split = Mesh(mesh.devices.reshape(tuple(SIZES.values())), tuple(SIZES))
    spec = P(ROW, COL)
    return jax.shard_map(body, mesh=split, in_specs=(spec,), out_specs=spec, check_vma=False)
```

```python
import functools
import math

import jax
import jax.numpy as jnp
from jax import lax
from jax.experimental import pallas as pl
from jax.experimental.pallas import tpu as pltpu
from jax.sharding import Mesh
from jax.sharding import PartitionSpec as P

D = 5632
F = 9216

first_term = 3.4445
third_term = -4.775
fifth_term = 2.0315

SIZES = {"y": 4, "xl": 2, "core": 2, "xh": 2, "z": 8}
ROW = ("y", "xl", "core")
COL = ("xh", "z")
BF = jnp.bfloat16
CUT = 256

SMEM_SPEC = pl.BlockSpec(memory_space=pltpu.SMEM)
VMEM_SPEC = pl.BlockSpec(memory_space=pltpu.VMEM)
NEAR = (0, 1, 2, 3, 5, 6, 7)
EARLY = [(0, 0), (1, 0), (3, 0), (0, 1)]
ORDER = EARLY + [(2, 0), (1, 1), (3, 1), (2, 1)]
FIRST = [(*at, dcore) for at in EARLY for dcore in range(2)]
SECOND = [(*at, dcore) for at in ORDER[4:] for dcore in range(2)]
LAST_DIMS = (((1,), (1,)), ((), ()))


def params(mib):
    return pltpu.CompilerParams(vmem_limit_bytes=mib * 2**20)


def shift(value, axis, by):
    n = SIZES[axis]
    return lax.ppermute(value, axis, [(i, (i + by) % n) for i in range(n)])


def after(values, *marks):
    return lax.optimization_barrier((*values, *marks))[: len(values)]


def row_gather(own):
    got = {(0, 0): own}
    up, down = shift(own, "y", 1), shift(own, "y", -1)
    got[3, 0], got[1, 0] = up, down
    got[0, 1] = shift(own, "xl", 1)
    got[3, 1], got[1, 1] = shift(up, "xl", 1), shift(down, "xl", 1)
    here, across = after((own, got[0, 1]), up, down)
    got[2, 0], got[2, 1] = shift(here, "y", 2), shift(across, "y", 2)
    blocks = {(*at, 0): got[at] for at in ORDER}
    for at, block in zip(EARLY, after([got[at] for at in EARLY], got[2, 0])):
        blocks[*at, 1] = shift(block, "core", 1)
    for at in ORDER[4:]:
        blocks[*at, 1] = shift(got[at], "core", 1)
    return blocks


def by_slot(blocks):
    return [blocks[dy, dxl, dcore] for dxl in range(2) for dy in range(4) for dcore in range(2)]


def tn(left, right):
    return lax.dot_general(left, right, (((0,), (0,)), ((), ())), preferred_element_type=jnp.float32)


def early_kernel(own, *refs):
    blocks, out = refs[:-1], refs[-1]
    for i, block in enumerate(blocks):
        out[i] = tn(own[...], block[...]).astype(BF)


def late_kernel(at, own, done, *refs):
    blocks, outs, hold = refs[:-19], refs[-19:-1], refs[-1]
    tiles = [done[i] for i in range(done.shape[0])]
    for block in blocks:
        tiles.append(tn(own[...], block[...]).astype(BF))
    for i, (dy, dxl, dcore) in enumerate(FIRST + SECOND):
        hold[lax.rem(dy * 2 + dcore + 8 - at[0], 8), dxl] = tiles[i]
    chunks = ((outs[:9], pl.ds(0, CUT)), (outs[9:], pl.ds(CUT, own.shape[1] - CUT)))
    for to, rows in chunks:
        for i, d in enumerate(NEAR):
            to[i][...] = hold[d, :, rows, :]
        for h in range(2):
            to[7 + h][...] = hold[4, h, rows, :]


def gram_cost(n, m):
    return pl.CostEstimate(flops=16 * n * n * m, bytes_accessed=10_000_000, transcendentals=0)


def early_tiles(own, blocks):
    m, n = own.shape
    return pl.pallas_call(
        early_kernel,
        out_shape=jax.ShapeDtypeStruct((len(blocks), n, n), BF),
        in_specs=[VMEM_SPEC] * (1 + len(blocks)),
        out_specs=VMEM_SPEC,
        compiler_params=params(16),
        cost_estimate=gram_cost(n, m),
    )(own, *blocks)


def gram_tiles(z, own, done, blocks):
    m, n = own.shape
    out_shape = []
    for rows in (CUT, n - CUT):
        out_shape += [jax.ShapeDtypeStruct((2, rows, n), BF)] * 7 + [jax.ShapeDtypeStruct((rows, n), BF)] * 2
    outs = pl.pallas_call(
        late_kernel,
        out_shape=out_shape,
        in_specs=[SMEM_SPEC] + [VMEM_SPEC] * (2 + len(blocks)),
        out_specs=[VMEM_SPEC] * 18,
        scratch_shapes=[pltpu.VMEM((8, 2, n, n), BF)],
        compiler_params=params(22),
        cost_estimate=gram_cost(n, m),
    )(z, own, done, *blocks)
    return outs[:9], outs[9:]


def add(*terms):
    return sum(t.astype(jnp.float32) for t in terms)


def ring_sum(tiles):
    near, far_up, far_down = dict(zip(NEAR, tiles[:7])), tiles[7], tiles[8]
    up, down = shift(far_up, "z", 1), shift(far_down, "z", -1)
    up = jnp.stack([add(near[3][0], up).astype(BF), near[3][1]])
    down = jnp.stack([near[5][0], add(near[5][1], down).astype(BF)])
    up, down = shift(up, "z", 1), shift(down, "z", -1)
    for d in (2, 1):
        up = shift(add(near[d], up).astype(BF), "z", 1)
        down = shift(add(near[8 - d], down).astype(BF), "z", -1)
    total = add(near[0], up, down)
    return (total + shift(total.astype(BF), "xh", 1).astype(jnp.float32)).astype(BF)


def ring_gather(pair):
    got = [pair] + [None] * 7
    for s in (1, 2, 3):
        got[8 - s] = shift(got[(9 - s) % 8], "z", 1)
        got[s] = shift(got[s - 1], "z", -1)
    return got[:4] + got[5:] + [shift(got[5][0], "z", 1), shift(got[3][1], "z", -1)]


def nt(left, right):
    return lax.dot_general(left, right, LAST_DIMS, preferred_element_type=jnp.float32)


def near_kernel(at, *refs):
    blocks, tiles, (y, gram) = refs[:16], refs[16:23], refs[23:]
    for h in range(2):
        for i, d in enumerate(NEAR):
            gram[h * 8 + lax.rem(at[0] + d, 8)] = tiles[i][h]
        gram[h * 8 + lax.rem(at[0] + 4, 8)] = jnp.zeros(gram.shape[1:], BF)
    total = None
    for j in range(16):
        part = nt(blocks[j][...], gram[j])
        total = part if total is None else total + part
    y[...] = total


def far_kernel(at, *refs):
    blocks, (far_0, far_1, part, y, y_half) = refs[:16], refs[16:]
    for j in range(8):

        @pl.when(lax.rem(at[0] + 4, 8) == j)
        def _():
            total = part[...] + nt(blocks[j][...], far_0[...]) + nt(blocks[8 + j][...], far_1[...])
            y[...] = total
            y_half[...] = total.astype(BF)


def first_product(z, blocks, tiles):
    m, n = blocks[0].shape
    w = tiles[0].shape[1]
    part, gram = pl.pallas_call(
        near_kernel,
        out_shape=[jax.ShapeDtypeStruct((m, w), jnp.float32), jax.ShapeDtypeStruct((16, w, n), BF)],
        in_specs=[SMEM_SPEC] + [VMEM_SPEC] * 23,
        out_specs=[VMEM_SPEC] * 2,
        compiler_params=params(20),
        cost_estimate=pl.CostEstimate(flops=32 * n * w * m, bytes_accessed=10_000_000, transcendentals=0),
    )(z, *blocks, *tiles[:7])
    y, y_half = pl.pallas_call(
        far_kernel,
        out_shape=[jax.ShapeDtypeStruct((m, w), jnp.float32), jax.ShapeDtypeStruct((m, w), BF)],
        in_specs=[SMEM_SPEC] + [VMEM_SPEC] * 19,
        out_specs=[VMEM_SPEC] * 2,
        compiler_params=params(20),
        cost_estimate=pl.CostEstimate(flops=4 * n * w * m, bytes_accessed=3_000_000, transcendentals=0),
    )(z, *blocks, *tiles[7:], part)
    return y, y_half, (gram, *tiles[7:])


def last_kernel(lanes, final, at, *refs):
    blocks, grams, refs = refs[:16], (refs[16:19], refs[19:22]), refs[22:]
    sums = []
    for gram, *far in grams:
        total = None
        for j in range(16):
            is_far = lax.rem(at[0] + 4, 8) == j % 8
            right = jnp.where(is_far, far[j // 8][:, lanes], gram[j, :, lanes])
            part = nt(blocks[j][...], right)
            total = part if total is None else total + part
        sums.append(total)
    if final:
        x, y_a, y_b, acc_a, acc_b, out = refs
        scale = 0.2 * math.sqrt(max(D, F))
        for total, acc, y, cols in ((sums[0], acc_a, y_a, pl.ds(0, CUT)), (sums[1], acc_b, y_b, pl.ds(CUT, y_b.shape[1]))):
            square = acc[...] + total
            mixed = first_term * x[:, cols].astype(jnp.float32) + third_term * y[...] + fifth_term * square
            out[:, cols] = (scale * mixed).astype(out.dtype)
    else:
        refs[0][...], refs[1][...] = sums


def last_product(z, blocks, grams, start, extra=()):
    m, w = blocks[0].shape
    widths = [g[0].shape[1] for g in grams]
    final = bool(extra)
    shapes = [jax.ShapeDtypeStruct((m, v), jnp.float32) for v in widths]
    return pl.pallas_call(
        functools.partial(last_kernel, pl.ds(start, w), final),
        out_shape=jax.ShapeDtypeStruct((m, sum(widths)), BF) if final else shapes,
        in_specs=[SMEM_SPEC] + [VMEM_SPEC] * (22 + len(extra)),
        out_specs=VMEM_SPEC if final else [VMEM_SPEC] * 2,
        compiler_params=params(20),
        cost_estimate=pl.CostEstimate(flops=32 * w * sum(widths) * m, bytes_accessed=10_000_000, transcendentals=0),
    )(z, *blocks, *grams[0], *grams[1], *extra)


def body(iterate):
    z = jnp.reshape(lax.axis_index("z"), (1,)).astype(jnp.int32)
    xt, z = lax.optimization_barrier((iterate.T, z))
    blocks = row_gather(xt)
    done = early_tiles(xt, [blocks[at] for at in FIRST])
    tiles_a, tiles_b = gram_tiles(z, xt, done, [blocks[at] for at in SECOND])
    blocks = by_slot(blocks)
    sum_a = ring_sum(tiles_a)
    sum_b = ring_sum(tiles_b)
    all_a = ring_gather(sum_a)
    all_b = ring_gather(after((sum_b,), all_a[2], all_a[5])[0])
    y_a, half_a, gram_a = first_product(z, blocks, all_a)
    y_b, half_b, gram_b = first_product(z, blocks, all_b)
    grams = (gram_a, gram_b)
    got_a = row_gather(half_a)
    got_b = row_gather(after((half_b,), got_a[2, 0, 0])[0])
    sums = last_product(z, by_slot(got_a), grams, 0)
    return last_product(z, by_slot(got_b), grams, CUT, (xt, y_a, y_b, *sums)).T


def solution(mesh):
    split = Mesh(mesh.devices.reshape(tuple(SIZES.values())), tuple(SIZES))
    spec = P(ROW, COL)
    return jax.shard_map(body, mesh=split, in_specs=(spec,), out_specs=spec, check_vma=False)
```

```python
import functools
import math

import jax
import jax.numpy as jnp
from jax import lax
from jax.experimental import pallas as pl
from jax.experimental.pallas import tpu as pltpu
from jax.sharding import Mesh
from jax.sharding import PartitionSpec as P

D = 5632
F = 9216

first_term = 3.4445
third_term = -4.775
fifth_term = 2.0315

SIZES = {"y": 4, "xl": 2, "core": 2, "xh": 2, "z": 8}
ROW = ("y", "xl", "core")
COL = ("xh", "z")
BF = jnp.bfloat16
CUT = 256

SMEM_SPEC = pl.BlockSpec(memory_space=pltpu.SMEM)
VMEM_SPEC = pl.BlockSpec(memory_space=pltpu.VMEM)
NEAR = (0, 1, 2, 3, 5, 6, 7)
LAST_DIMS = (((1,), (1,)), ((), ()))


def params(mib):
    return pltpu.CompilerParams(vmem_limit_bytes=mib * 2**20)


def shift(value, axis, by):
    n = SIZES[axis]
    return lax.ppermute(value, axis, [(i, (i + by) % n) for i in range(n)])


def after(values, *marks):
    return lax.optimization_barrier((*values, *marks))[: len(values)]


def near_pairs(own):
    across = shift(own, "xl", 1)
    return [jnp.stack([own, across]), jnp.stack([shift(own, "y", 1), shift(own, "y", -1)])]


def far_pairs(near):
    return [shift(near[0], "y", 2), shift(near[1], "xl", 1)]


def both_cores(pairs):
    return [part for pair in pairs for part in (pair, shift(pair, "core", 1))]


def tn(left, right):
    return lax.dot_general(left, right, (((0,), (0,)), ((), ())), preferred_element_type=jnp.float32)


def gram_kernel(at, own, *refs):
    blocks, outs, hold = refs[:4], refs[4:12], refs[12]
    for j in range(8):
        hold[lax.rem(j + 8 - at[0], 8)] = tn(own[...], blocks[j // 2][j % 2]).astype(BF)
    for d in range(8):
        outs[d][...] = hold[d]


def gram_tiles(z, own, blocks):
    m, n = own.shape
    return pl.pallas_call(
        gram_kernel,
        out_shape=[jax.ShapeDtypeStruct((n, n), BF)] * 8,
        in_specs=[SMEM_SPEC] + [VMEM_SPEC] * 5,
        out_specs=[VMEM_SPEC] * 8,
        scratch_shapes=[pltpu.VMEM((8, n, n), BF)],
        compiler_params=params(20),
        cost_estimate=pl.CostEstimate(flops=16 * n * n * m, bytes_accessed=10_000_000, transcendentals=0),
    )(z, own, *blocks)


def add(*terms):
    return sum(t.astype(jnp.float32) for t in terms)


def ring_start(tiles, far_up):
    return shift(tiles[4 if far_up else 3], "z", 1), shift(tiles[5 if far_up else 4], "z", -1)


def ring_sum(tiles, far_up, up, down):
    for d in (3, 2, 1):
        if d < 3 or far_up:
            up = shift(add(tiles[d], up).astype(BF), "z", 1)
        if d < 3 or not far_up:
            down = shift(add(tiles[8 - d], down).astype(BF), "z", -1)
    return add(tiles[0], up, down)


def xh_sum(pair):
    return (pair + shift(pair.astype(BF), "xh", 1).astype(jnp.float32)).astype(BF)


def ring_step(got, s):
    got[8 - s] = shift(got[(9 - s) % 8], "z", 1)
    got[s] = shift(got[s - 1], "z", -1)


def ring_end(got):
    return got[:4] + got[5:] + [shift(got[5][0], "z", 1), shift(got[3][1], "z", -1)]


def hold(got, s, other, t):
    got[8 - s], got[s] = after((got[8 - s], got[s]), other[8 - t], other[t])


def ring_gathers(pair):
    got_a, got_b = [pair[:, :CUT]] + [None] * 7, [pair[:, CUT:]] + [None] * 7
    ring_step(got_a, 1)
    (got_b[0],) = after((got_b[0],), got_a[7], got_a[1])
    ring_step(got_b, 1)
    ring_step(got_a, 2)
    ring_step(got_a, 3)
    hold(got_a, 3, got_b, 1)
    all_a = ring_end(got_a)
    ring_step(got_b, 2)
    ring_step(got_b, 3)
    return all_a, ring_end(got_b)


def nt(left, right):
    return lax.dot_general(left, right, LAST_DIMS, preferred_element_type=jnp.float32)


def near_kernel(at, *refs):
    blocks, tiles, (y, gram) = refs[:8], refs[8:15], refs[15:]
    for h in range(2):
        for i, d in enumerate(NEAR):
            gram[h * 8 + lax.rem(at[0] + d, 8)] = tiles[i][h]
        gram[h * 8 + lax.rem(at[0] + 4, 8)] = jnp.zeros(gram.shape[1:], BF)
    total = None
    for j in range(16):
        part = nt(blocks[j // 2][j % 2], gram[j])
        total = part if total is None else total + part
    y[...] = total


def far_kernel(at, *refs):
    blocks, (far_0, far_1, part, y, y_half) = refs[:8], refs[8:]
    for j in range(8):

        @pl.when(lax.rem(at[0] + 4, 8) == j)
        def _():
            total = part[...] + nt(blocks[j // 2][j % 2], far_0[...]) + nt(blocks[4 + j // 2][j % 2], far_1[...])
            y[...] = total
            y_half[...] = total.astype(BF)


def first_product(z, blocks, tiles):
    _, m, n = blocks[0].shape
    w = tiles[0].shape[1]
    part, gram = pl.pallas_call(
        near_kernel,
        out_shape=[jax.ShapeDtypeStruct((m, w), jnp.float32), jax.ShapeDtypeStruct((16, w, n), BF)],
        in_specs=[SMEM_SPEC] + [VMEM_SPEC] * 15,
        out_specs=[VMEM_SPEC] * 2,
        compiler_params=params(20),
        cost_estimate=pl.CostEstimate(flops=32 * n * w * m, bytes_accessed=10_000_000, transcendentals=0),
    )(z, *blocks, *tiles[:7])
    y, y_half = pl.pallas_call(
        far_kernel,
        out_shape=[jax.ShapeDtypeStruct((m, w), jnp.float32), jax.ShapeDtypeStruct((m, w), BF)],
        in_specs=[SMEM_SPEC] + [VMEM_SPEC] * 11,
        out_specs=[VMEM_SPEC] * 2,
        compiler_params=params(20),
        cost_estimate=pl.CostEstimate(flops=4 * n * w * m, bytes_accessed=3_000_000, transcendentals=0),
    )(z, *blocks, *tiles[7:], part)
    return y, y_half, (gram, *tiles[7:])


def last_kernel(lanes, final, at, *refs):
    blocks, grams, refs = refs[:8], (refs[8:11], refs[11:14]), refs[14:]
    sums = []
    for gram, *far in grams:
        total = None
        for j in range(16):
            is_far = lax.rem(at[0] + 4, 8) == j % 8
            right = jnp.where(is_far, far[j // 8][:, lanes], gram[j, :, lanes])
            part = nt(blocks[j // 2][j % 2], right)
            total = part if total is None else total + part
        sums.append(total)
    if final:
        x, y_a, y_b, acc_a, acc_b, out = refs
        scale = 0.2 * math.sqrt(max(D, F))
        for total, acc, y, cols in ((sums[0], acc_a, y_a, pl.ds(0, CUT)), (sums[1], acc_b, y_b, pl.ds(CUT, y_b.shape[1]))):
            square = acc[...] + total
            mixed = first_term * x[:, cols].astype(jnp.float32) + third_term * y[...] + fifth_term * square
            out[:, cols] = (scale * mixed).astype(out.dtype)
    else:
        refs[0][...], refs[1][...] = sums


def last_product(z, blocks, grams, start, extra=()):
    _, m, w = blocks[0].shape
    widths = [g[0].shape[1] for g in grams]
    final = bool(extra)
    shapes = [jax.ShapeDtypeStruct((m, v), jnp.float32) for v in widths]
    return pl.pallas_call(
        functools.partial(last_kernel, pl.ds(start, w), final),
        out_shape=jax.ShapeDtypeStruct((m, sum(widths)), BF) if final else shapes,
        in_specs=[SMEM_SPEC] + [VMEM_SPEC] * (14 + len(extra)),
        out_specs=VMEM_SPEC if final else [VMEM_SPEC] * 2,
        compiler_params=params(20),
        cost_estimate=pl.CostEstimate(flops=32 * w * sum(widths) * m, bytes_accessed=10_000_000, transcendentals=0),
    )(z, *blocks, *grams[0], *grams[1], *extra)


def body(iterate):
    z = jnp.reshape(lax.axis_index("z"), (1,)).astype(jnp.int32)
    xt, z = lax.optimization_barrier((iterate.T, z))
    near = near_pairs(xt)
    far = far_pairs(near)
    blocks = both_cores(near)
    early = gram_tiles(z, xt, blocks)
    sent = ring_start(early, True)
    blocks += both_cores(after(far, *sent))
    late = gram_tiles(z, xt, blocks[4:])
    pair = jnp.stack([ring_sum(early, True, *sent), ring_sum(late, False, *ring_start(late, False))])
    pair = xh_sum(pair)
    all_a, all_b = ring_gathers(pair)
    y_a, half_a, gram_a = first_product(z, blocks, all_a)
    y_b, half_b, gram_b = first_product(z, blocks, all_b)
    grams = (gram_a, gram_b)
    near_a = near_pairs(half_a)
    far_a = far_pairs(near_a)
    near_b = near_pairs(half_b)
    far_b = far_pairs(near_b)
    got_a = both_cores(near_a) + both_cores(after(far_a, near_b[1]))
    sums = last_product(z, got_a, grams, 0)
    got_b = both_cores(near_b) + both_cores(after(far_b, *sums))
    return last_product(z, got_b, grams, CUT, (xt, y_a, y_b, *sums)).T


def solution(mesh):
    split = Mesh(mesh.devices.reshape(tuple(SIZES.values())), tuple(SIZES))
    spec = P(ROW, COL)
    return jax.shard_map(body, mesh=split, in_specs=(spec,), out_specs=spec, check_vma=False)
```

```python
import functools
import math

import jax
import jax.numpy as jnp
from jax import lax
from jax.experimental import pallas as pl
from jax.experimental.pallas import tpu as pltpu
from jax.sharding import Mesh
from jax.sharding import PartitionSpec as P

D = 5632
F = 9216

first_term = 3.4445
third_term = -4.775
fifth_term = 2.0315

SIZES = {"y": 4, "xl": 2, "core": 2, "xh": 2, "z": 8}
ROW = ("y", "xl", "core")
COL = ("xh", "z")
BF = jnp.bfloat16
CUT = 256

SMEM_SPEC = pl.BlockSpec(memory_space=pltpu.SMEM)
VMEM_SPEC = pl.BlockSpec(memory_space=pltpu.VMEM)
NEAR = (0, 1, 2, 3, 5, 6, 7)
LAST_DIMS = (((1,), (1,)), ((), ()))


def params(mib):
    return pltpu.CompilerParams(vmem_limit_bytes=mib * 2**20)


def shift(value, axis, by):
    n = SIZES[axis]
    return lax.ppermute(value, axis, [(i, (i + by) % n) for i in range(n)])


def after(values, *marks):
    return lax.optimization_barrier((*values, *marks))[: len(values)]


def near_pairs(own):
    across = shift(own, "xl", 1)
    return [jnp.stack([own, across]), jnp.stack([shift(own, "y", 1), shift(own, "y", -1)])]


def far_pairs(near):
    return [shift(near[0], "y", 2), shift(near[1], "xl", 1)]


def both_cores(pairs):
    return [part for pair in pairs for part in (pair, shift(pair, "core", 1))]


def tn(left, right):
    return lax.dot_general(left, right, (((0,), (0,)), ((), ())), preferred_element_type=jnp.float32)


def gram_kernel(at, own, *refs):
    blocks, outs, hold = refs[:4], refs[4:12], refs[12]
    for j in range(8):
        hold[lax.rem(j + 8 - at[0], 8)] = tn(own[...], blocks[j // 2][j % 2]).astype(BF)
    for d in range(8):
        outs[d][...] = hold[d]


def gram_tiles(z, own, blocks):
    m, n = own.shape
    return pl.pallas_call(
        gram_kernel,
        out_shape=[jax.ShapeDtypeStruct((n, n), BF)] * 8,
        in_specs=[SMEM_SPEC] + [VMEM_SPEC] * 5,
        out_specs=[VMEM_SPEC] * 8,
        scratch_shapes=[pltpu.VMEM((8, n, n), BF)],
        compiler_params=params(20),
        cost_estimate=pl.CostEstimate(flops=16 * n * n * m, bytes_accessed=10_000_000, transcendentals=0),
    )(z, own, *blocks)


def add(*terms):
    return sum(t.astype(jnp.float32) for t in terms)


def ring_start(tiles, far_up):
    return shift(tiles[4 if far_up else 3], "z", 1), shift(tiles[5 if far_up else 4], "z", -1)


def ring_sum(tiles, far_up, up, down):
    for d in (3, 2, 1):
        if d < 3 or far_up:
            up = shift(add(tiles[d], up).astype(BF), "z", 1)
        if d < 3 or not far_up:
            down = shift(add(tiles[8 - d], down).astype(BF), "z", -1)
    return add(tiles[0], up, down)


def xh_sum(pair):
    return (pair + shift(pair.astype(BF), "xh", 1).astype(jnp.float32)).astype(BF)


def ring_step(got, s):
    got[8 - s] = shift(got[(9 - s) % 8], "z", 1)
    got[s] = shift(got[s - 1], "z", -1)


def ring_end(got):
    return got[:4] + got[5:] + [shift(got[5][0], "z", 1), shift(got[3][1], "z", -1)]


def hold(got, s, other, t):
    got[8 - s], got[s] = after((got[8 - s], got[s]), other[8 - t], other[t])


def ring_gathers(pair):
    got_a, got_b = [xh_sum(pair[:, :CUT])] + [None] * 7, [None] * 8
    ring_step(got_a, 1)
    (got_b[0],) = after((xh_sum(pair[:, CUT:]),), got_a[7], got_a[1])
    ring_step(got_b, 1)
    ring_step(got_a, 2)
    ring_step(got_a, 3)
    hold(got_a, 3, got_b, 1)
    all_a = ring_end(got_a)
    ring_step(got_b, 2)
    ring_step(got_b, 3)
    return all_a, ring_end(got_b)


def nt(left, right):
    return lax.dot_general(left, right, LAST_DIMS, preferred_element_type=jnp.float32)


def near_kernel(at, *refs):
    blocks, tiles, (y, gram) = refs[:8], refs[8:15], refs[15:]
    for h in range(2):
        for i, d in enumerate(NEAR):
            gram[h * 8 + lax.rem(at[0] + d, 8)] = tiles[i][h]
        gram[h * 8 + lax.rem(at[0] + 4, 8)] = jnp.zeros(gram.shape[1:], BF)
    total = None
    for j in range(16):
        part = nt(blocks[j // 2][j % 2], gram[j])
        total = part if total is None else total + part
    y[...] = total


def far_kernel(at, *refs):
    blocks, (far_0, far_1, part, y, y_half) = refs[:8], refs[8:]
    for j in range(8):

        @pl.when(lax.rem(at[0] + 4, 8) == j)
        def _():
            total = part[...] + nt(blocks[j // 2][j % 2], far_0[...]) + nt(blocks[4 + j // 2][j % 2], far_1[...])
            y[...] = total
            y_half[...] = total.astype(BF)


def first_product(z, blocks, tiles):
    _, m, n = blocks[0].shape
    w = tiles[0].shape[1]
    part, gram = pl.pallas_call(
        near_kernel,
        out_shape=[jax.ShapeDtypeStruct((m, w), jnp.float32), jax.ShapeDtypeStruct((16, w, n), BF)],
        in_specs=[SMEM_SPEC] + [VMEM_SPEC] * 15,
        out_specs=[VMEM_SPEC] * 2,
        compiler_params=params(20),
        cost_estimate=pl.CostEstimate(flops=32 * n * w * m, bytes_accessed=10_000_000, transcendentals=0),
    )(z, *blocks, *tiles[:7])
    y, y_half = pl.pallas_call(
        far_kernel,
        out_shape=[jax.ShapeDtypeStruct((m, w), jnp.float32), jax.ShapeDtypeStruct((m, w), BF)],
        in_specs=[SMEM_SPEC] + [VMEM_SPEC] * 11,
        out_specs=[VMEM_SPEC] * 2,
        compiler_params=params(20),
        cost_estimate=pl.CostEstimate(flops=4 * n * w * m, bytes_accessed=3_000_000, transcendentals=0),
    )(z, *blocks, *tiles[7:], part)
    return y, y_half, (gram, *tiles[7:])


def last_kernel(lanes, final, at, *refs):
    blocks, grams, refs = refs[:8], (refs[8:11], refs[11:14]), refs[14:]
    sums = []
    for gram, *far in grams:
        total = None
        for j in range(16):
            is_far = lax.rem(at[0] + 4, 8) == j % 8
            right = jnp.where(is_far, far[j // 8][:, lanes], gram[j, :, lanes])
            part = nt(blocks[j // 2][j % 2], right)
            total = part if total is None else total + part
        sums.append(total)
    if final:
        x, y_a, y_b, acc_a, acc_b, out = refs
        scale = 0.2 * math.sqrt(max(D, F))
        for total, acc, y, cols in ((sums[0], acc_a, y_a, pl.ds(0, CUT)), (sums[1], acc_b, y_b, pl.ds(CUT, y_b.shape[1]))):
            square = acc[...] + total
            mixed = first_term * x[:, cols].astype(jnp.float32) + third_term * y[...] + fifth_term * square
            out[:, cols] = (scale * mixed).astype(out.dtype)
    else:
        refs[0][...], refs[1][...] = sums


def last_product(z, blocks, grams, start, extra=()):
    _, m, w = blocks[0].shape
    widths = [g[0].shape[1] for g in grams]
    final = bool(extra)
    shapes = [jax.ShapeDtypeStruct((m, v), jnp.float32) for v in widths]
    return pl.pallas_call(
        functools.partial(last_kernel, pl.ds(start, w), final),
        out_shape=jax.ShapeDtypeStruct((m, sum(widths)), BF) if final else shapes,
        in_specs=[SMEM_SPEC] + [VMEM_SPEC] * (14 + len(extra)),
        out_specs=VMEM_SPEC if final else [VMEM_SPEC] * 2,
        compiler_params=params(20),
        cost_estimate=pl.CostEstimate(flops=32 * w * sum(widths) * m, bytes_accessed=10_000_000, transcendentals=0),
    )(z, *blocks, *grams[0], *grams[1], *extra)


def body(iterate):
    z = jnp.reshape(lax.axis_index("z"), (1,)).astype(jnp.int32)
    xt, z = lax.optimization_barrier((iterate.T, z))
    near = near_pairs(xt)
    far = far_pairs(near)
    blocks = both_cores(near)
    early = gram_tiles(z, xt, blocks)
    sent = ring_start(early, True)
    blocks += both_cores(after(far, *sent))
    late = gram_tiles(z, xt, blocks[4:])
    pair = jnp.stack([ring_sum(early, True, *sent), ring_sum(late, False, *ring_start(late, False))])
    all_a, all_b = ring_gathers(pair)
    y_a, half_a, gram_a = first_product(z, blocks, all_a)
    y_b, half_b, gram_b = first_product(z, blocks, all_b)
    grams = (gram_a, gram_b)
    near_a = near_pairs(half_a)
    far_a = far_pairs(near_a)
    near_b = near_pairs(half_b)
    far_b = far_pairs(near_b)
    got_a = both_cores(after(near_a + far_a, *near_b))
    sums = last_product(z, got_a, grams, 0)
    got_b = both_cores(near_b) + both_cores(after(far_b, *sums))
    return last_product(z, got_b, grams, CUT, (xt, y_a, y_b, *sums)).T


def solution(mesh):
    split = Mesh(mesh.devices.reshape(tuple(SIZES.values())), tuple(SIZES))
    spec = P(ROW, COL)
    return jax.shard_map(body, mesh=split, in_specs=(spec,), out_specs=spec, check_vma=False)
```

```python
import functools
import math

import jax
import jax.numpy as jnp
from jax import lax
from jax.experimental import pallas as pl
from jax.experimental.pallas import tpu as pltpu
from jax.sharding import Mesh
from jax.sharding import PartitionSpec as P

D = 5632
F = 9216

first_term = 3.4445
third_term = -4.775
fifth_term = 2.0315

SIZES = {"y": 4, "xl": 2, "core": 2, "xh": 2, "z": 8}
ROW = ("y", "xl", "core")
COL = ("xh", "z")
BF = jnp.bfloat16
CUT = 256

SMEM_SPEC = pl.BlockSpec(memory_space=pltpu.SMEM)
VMEM_SPEC = pl.BlockSpec(memory_space=pltpu.VMEM)
NEAR = (0, 1, 2, 3, 5, 6, 7)
LAST_DIMS = (((1,), (1,)), ((), ()))


def params(mib):
    return pltpu.CompilerParams(vmem_limit_bytes=mib * 2**20)


def shift(value, axis, by):
    n = SIZES[axis]
    return lax.ppermute(value, axis, [(i, (i + by) % n) for i in range(n)])


def after(values, *marks):
    return lax.optimization_barrier((*values, *marks))[: len(values)]


def near_pairs(own):
    across = shift(own, "xl", 1)
    return [jnp.stack([own, across]), jnp.stack([shift(own, "y", 1), shift(own, "y", -1)])]


def far_pairs(near):
    return [shift(near[0], "y", 2), shift(near[1], "xl", 1)]


def both_cores(pairs):
    return [part for pair in pairs for part in (pair, shift(pair, "core", 1))]


def tn(left, right):
    return lax.dot_general(left, right, (((0,), (0,)), ((), ())), preferred_element_type=jnp.float32)


def gram_kernel(at, own, *refs):
    blocks, outs, hold = refs[:4], refs[4:12], refs[12]
    for j in range(8):
        hold[lax.rem(j + 8 - at[0], 8)] = tn(own[...], blocks[j // 2][j % 2]).astype(BF)
    for d in range(8):
        outs[d][...] = hold[d]


def gram_tiles(z, own, blocks):
    m, n = own.shape
    return pl.pallas_call(
        gram_kernel,
        out_shape=[jax.ShapeDtypeStruct((n, n), BF)] * 8,
        in_specs=[SMEM_SPEC] + [VMEM_SPEC] * 5,
        out_specs=[VMEM_SPEC] * 8,
        scratch_shapes=[pltpu.VMEM((8, n, n), BF)],
        compiler_params=params(20),
        cost_estimate=pl.CostEstimate(flops=16 * n * n * m, bytes_accessed=10_000_000, transcendentals=0),
    )(z, own, *blocks)


def add(*terms):
    return sum(t.astype(jnp.float32) for t in terms)


def ring_start(tiles, far_up):
    return shift(tiles[4 if far_up else 3], "z", 1), shift(tiles[5 if far_up else 4], "z", -1)


def ring_sum(tiles, far_up, up, down):
    for d in (3, 2, 1):
        if d < 3 or far_up:
            up = shift(add(tiles[d], up).astype(BF), "z", 1)
        if d < 3 or not far_up:
            down = shift(add(tiles[8 - d], down).astype(BF), "z", -1)
    return add(tiles[0], up, down)


def xh_sum(pair):
    return (pair + shift(pair.astype(BF), "xh", 1).astype(jnp.float32)).astype(BF)


def ring_step(got, s):
    got[8 - s] = shift(got[(9 - s) % 8], "z", 1)
    got[s] = shift(got[s - 1], "z", -1)


def ring_end(got):
    return got[:4] + got[5:] + [shift(got[5][0], "z", 1), shift(got[3][1], "z", -1)]


def hold(got, s, other, t):
    got[8 - s], got[s] = after((got[8 - s], got[s]), other[8 - t], other[t])


def ring_gathers(pair):
    got_a, got_b = [xh_sum(pair[:, :CUT])] + [None] * 7, [None] * 8
    ring_step(got_a, 1)
    (got_b[0],) = after((xh_sum(pair[:, CUT:]),), got_a[7], got_a[1])
    ring_step(got_b, 1)
    ring_step(got_a, 2)
    ring_step(got_a, 3)
    hold(got_a, 3, got_b, 1)
    all_a = ring_end(got_a)
    hold(got_b, 1, got_a, 3)
    ring_step(got_b, 2)
    ring_step(got_b, 3)
    return all_a, ring_end(got_b)


def nt(left, right):
    return lax.dot_general(left, right, LAST_DIMS, preferred_element_type=jnp.float32)


def near_kernel(at, *refs):
    blocks, tiles, (y, gram) = refs[:8], refs[8:15], refs[15:]
    for h in range(2):
        for i, d in enumerate(NEAR):
            gram[h * 8 + lax.rem(at[0] + d, 8)] = tiles[i][h]
        gram[h * 8 + lax.rem(at[0] + 4, 8)] = jnp.zeros(gram.shape[1:], BF)
    total = None
    for j in range(16):
        part = nt(blocks[j // 2][j % 2], gram[j])
        total = part if total is None else total + part
    y[...] = total


def far_kernel(at, *refs):
    blocks, (far_0, far_1, part, y, y_half) = refs[:8], refs[8:]
    for j in range(8):

        @pl.when(lax.rem(at[0] + 4, 8) == j)
        def _():
            total = part[...] + nt(blocks[j // 2][j % 2], far_0[...]) + nt(blocks[4 + j // 2][j % 2], far_1[...])
            y[...] = total
            y_half[...] = total.astype(BF)


def first_product(z, blocks, tiles):
    _, m, n = blocks[0].shape
    w = tiles[0].shape[1]
    part, gram = pl.pallas_call(
        near_kernel,
        out_shape=[jax.ShapeDtypeStruct((m, w), jnp.float32), jax.ShapeDtypeStruct((16, w, n), BF)],
        in_specs=[SMEM_SPEC] + [VMEM_SPEC] * 15,
        out_specs=[VMEM_SPEC] * 2,
        compiler_params=params(20),
        cost_estimate=pl.CostEstimate(flops=32 * n * w * m, bytes_accessed=10_000_000, transcendentals=0),
    )(z, *blocks, *tiles[:7])
    y, y_half = pl.pallas_call(
        far_kernel,
        out_shape=[jax.ShapeDtypeStruct((m, w), jnp.float32), jax.ShapeDtypeStruct((m, w), BF)],
        in_specs=[SMEM_SPEC] + [VMEM_SPEC] * 11,
        out_specs=[VMEM_SPEC] * 2,
        compiler_params=params(20),
        cost_estimate=pl.CostEstimate(flops=4 * n * w * m, bytes_accessed=3_000_000, transcendentals=0),
    )(z, *blocks, *tiles[7:], part)
    return y, y_half, (gram, *tiles[7:])


def last_kernel(lanes, final, at, *refs):
    blocks, grams, refs = refs[:8], (refs[8:11], refs[11:14]), refs[14:]
    sums = []
    for gram, *far in grams:
        total = None
        for j in range(16):
            is_far = lax.rem(at[0] + 4, 8) == j % 8
            right = jnp.where(is_far, far[j // 8][:, lanes], gram[j, :, lanes])
            part = nt(blocks[j // 2][j % 2], right)
            total = part if total is None else total + part
        sums.append(total)
    if final:
        x, y_a, y_b, acc_a, acc_b, out = refs
        scale = 0.2 * math.sqrt(max(D, F))
        for total, acc, y, cols in ((sums[0], acc_a, y_a, pl.ds(0, CUT)), (sums[1], acc_b, y_b, pl.ds(CUT, y_b.shape[1]))):
            square = acc[...] + total
            mixed = first_term * x[:, cols].astype(jnp.float32) + third_term * y[...] + fifth_term * square
            out[:, cols] = (scale * mixed).astype(out.dtype)
    else:
        refs[0][...], refs[1][...] = sums


def last_product(z, blocks, grams, start, extra=()):
    _, m, w = blocks[0].shape
    widths = [g[0].shape[1] for g in grams]
    final = bool(extra)
    shapes = [jax.ShapeDtypeStruct((m, v), jnp.float32) for v in widths]
    return pl.pallas_call(
        functools.partial(last_kernel, pl.ds(start, w), final),
        out_shape=jax.ShapeDtypeStruct((m, sum(widths)), BF) if final else shapes,
        in_specs=[SMEM_SPEC] + [VMEM_SPEC] * (14 + len(extra)),
        out_specs=VMEM_SPEC if final else [VMEM_SPEC] * 2,
        compiler_params=params(20),
        cost_estimate=pl.CostEstimate(flops=32 * w * sum(widths) * m, bytes_accessed=10_000_000, transcendentals=0),
    )(z, *blocks, *grams[0], *grams[1], *extra)


def body(iterate):
    z = jnp.reshape(lax.axis_index("z"), (1,)).astype(jnp.int32)
    xt, z = lax.optimization_barrier((iterate.T, z))
    near = near_pairs(xt)
    far = far_pairs(near)
    blocks = both_cores(near)
    early = gram_tiles(z, xt, blocks)
    sent = ring_start(early, True)
    blocks += both_cores(after(far, *sent))
    late = gram_tiles(z, xt, blocks[4:])
    pair = jnp.stack([ring_sum(early, True, *sent), ring_sum(late, False, *ring_start(late, False))])
    all_a, all_b = ring_gathers(pair)
    y_a, half_a, gram_a = first_product(z, blocks, all_a)
    y_b, half_b, gram_b = first_product(z, blocks, all_b)
    grams = (gram_a, gram_b)
    near_a = near_pairs(half_a)
    far_a = far_pairs(near_a)
    near_b = near_pairs(half_b)
    far_b = far_pairs(near_b)
    got_a = both_cores(after(near_a + far_a, *near_b))
    sums = last_product(z, got_a, grams, 0)
    got_b = both_cores(near_b) + both_cores(after(far_b, *sums))
    return last_product(z, got_b, grams, CUT, (xt, y_a, y_b, *sums)).T


def solution(mesh):
    split = Mesh(mesh.devices.reshape(tuple(SIZES.values())), tuple(SIZES))
    spec = P(ROW, COL)
    return jax.shard_map(body, mesh=split, in_specs=(spec,), out_specs=spec, check_vma=False)
```
